512 devices in a mesh: blk: 16 (over y, core), grp: 32 (over z, x).
Axes of the slice: x: 4, y: 8, z: 8, core: 2. Of those that a mesh axis runs over, the one named last changes fastest.
Arguments:
- int_table: bfloat16 [16384, 256], P('grp'), may hold values from -0.3984375 to 0.3984375
- dom_rows: int32 [8192, 256], P(('blk', 'grp')), may hold values from 0 to 16383, as said below
- pno_maps: bfloat16 [8192, 256, 128], P(('blk', 'grp')), may hold values from -0.375 to 0.375
- amplitudes: bfloat16 [8192, 128, 128], P(('blk', 'grp')), may hold values from -2.5 to 2.5
- pno_count: int32 [8192], P(('blk', 'grp')), may hold values from 32 to 128
- pno_energy: float32 [8192, 128], P(('blk', 'grp')), may hold values from 0.2 to 3
- occ_sum: float32 [8192], P(('blk', 'grp')), may hold values from -2 to -0.5
- partner_slot: int32 [8192, 6], P(('blk', 'grp')), may hold values from 0 to 47
- margin_index: int32 [8192, 6], P(('blk', 'grp')), may hold values from 0 to 31
- coupling_coef: float32 [8192, 6], P(('blk', 'grp')), may hold values from -0.4 to 0.4
- margin_pool: bfloat16 [1024, 128, 128], P('grp'), may hold values from -0.5 to 0.5
Outputs:
- residual: bfloat16 [8192, 128, 128], P(('blk', 'grp'))
The draws below stay inside these ranges and needn't reach their ends.
Inputs may be any that keep to these rules, and one draw needn't show every extreme that they name: `dom_rows`: id // 512 is the pair group whose slab holds the row. Among the 4096 entries of one device's pairs no group is named more than 256 times; in every cycle position one group is named exactly 256 times by each device of that position. `partner_slot`: slot w names pair w mod 16 of the slab at cycle position (own position + w // 16 - 1) mod 16 in the same group.
All inputs are finite; a program needn't handle non-finite values.
Results may differ from the reference program's by a relative error of at most 0.0025.
Values may be sent and summed in bfloat16 or wider, within the bound.
No kernel may reach another device: no remote copies, remote signals or barrier semaphores. Data moves between devices by JAX's collectives and lax.ppermute only.
A program may use at most 128 MiB of HBM per device.

```python
import jax
import jax.numpy as jnp
from jax import lax

P_SIZE = 128
V = 256
DOM = 256
NPART = 6
NOVL = 32
PAIRS_DEV = 16
PAIRS = 8192
ROWS_GRP = 512
N_BLK = 16
N_GRP = 32


def draw_dom_rows(key, part):
    key = jax.random.fold_in(key, 11)
    entries = PAIRS_DEV * DOM
    capacity = 2 * entries // N_GRP
    slot_total = N_GRP * capacity
    slab_total = N_BLK * N_GRP
    first_key, second_key, third_key = jax.random.split(key, 3)
    full_owner = jax.random.randint(first_key, (N_BLK,), 0, N_GRP)
    full_per_slab = jnp.repeat(full_owner, N_GRP)
    owner_of_slot = jnp.arange(slot_total, dtype=jnp.int32) // capacity

    def choose_owners(slab_key, favoured):
        shuffle_key, spread_key = jax.random.split(slab_key)
        shuffle = jax.random.permutation(shuffle_key, slot_total)
        scores = jnp.where(owner_of_slot == favoured, 0, 1 + shuffle)
        ranking = jnp.argsort(scores, stable=True)[:entries]
        chosen = owner_of_slot[ranking]
        return chosen[jax.random.permutation(spread_key, entries)]
    owners = jax.vmap(choose_owners)(jax.random.split(second_key, slab_total), full_per_slab)
    local_row = jax.random.randint(third_key, (slab_total, entries), 0, ROWS_GRP)
    row_ids = owners * ROWS_GRP + local_row
    return row_ids.reshape(slab_total * PAIRS_DEV, DOM).astype(jnp.int32)


def place_ends(values, rng, smallest, largest):
    longest = values.shape.index(max(values.shape))
    spots = []
    for shift in (0, 1):
        where = [jax.random.randint(jax.random.fold_in(rng, axis), (), 0, length) for axis, length in enumerate(values.shape)]
        where[longest] = (where[longest] + shift) % values.shape[longest]
        spots.append(tuple(where))
    return values.at[spots[0]].set(smallest).at[spots[1]].set(largest)


def level_of(rng, dims, shards, smallest, top_value):
    factor_of, own = 1.0, jax.random.fold_in(rng, 6)
    for dim, blocks in shards:
        steps = jnp.exp(jax.random.uniform(jax.random.fold_in(own, dim), (blocks,), jnp.float32, smallest / len(shards), top_value / len(shards)))
        factor_of = factor_of * jnp.repeat(steps, dims[dim] // blocks).reshape([-1 if axis == dim else 1 for axis in range(len(dims))])
    return factor_of


def noise(own_key, extent, scale, limit, pieces=(), kind=jnp.bfloat16):
    values = scale * jax.random.normal(own_key, extent, jnp.float32)
    if pieces:
        values = values * level_of(own_key, extent, pieces, -0.22, 0.18)
    return jnp.clip(values, -limit, limit).astype(kind)


def setup_inputs(seed: int = 0) -> dict:
    key_list = jax.random.split(jax.random.key(seed), 12)
    return {
        "int_table": noise(key_list[0], (ROWS_GRP * N_GRP, V), 0.0625, 0.3984375, ((0, 32),)),
        "dom_rows": draw_dom_rows(jax.random.fold_in(key_list[11], 71), 0),
        "pno_maps": noise(key_list[2], (PAIRS, V, P_SIZE), V ** -0.5, 0.375, ((0, 512),)),
        "amplitudes": noise(key_list[3], (PAIRS, P_SIZE, P_SIZE), 0.3, 2.5, ((0, 512),)),
        "pno_count": place_ends(jax.random.randint(key_list[4], (PAIRS,), P_SIZE // 4, P_SIZE + 1), jax.random.fold_in(key_list[4], 1), P_SIZE // 4, P_SIZE).astype(jnp.int32),
        "pno_energy": jnp.clip(0.2 + 2.8 * jax.random.uniform(key_list[5], (PAIRS, P_SIZE), jnp.float32) ** level_of(key_list[5], (PAIRS, P_SIZE), ((0, 512),), -0.2, 0.2), 0.2, 3.0),
        "occ_sum": jnp.clip(-2.0 + 1.5 * jax.random.uniform(key_list[6], (PAIRS,), jnp.float32) ** level_of(key_list[6], (PAIRS,), ((0, 512),), -0.2, 0.2), -2.0, -0.5),
        "partner_slot": place_ends(jax.random.randint(key_list[7], (PAIRS, NPART), 0, 3 * PAIRS_DEV), jax.random.fold_in(key_list[7], 1), 0, (3 * PAIRS_DEV) - 1).astype(jnp.int32),
        "margin_index": place_ends(jax.random.randint(key_list[8], (PAIRS, NPART), 0, NOVL), jax.random.fold_in(key_list[8], 1), 0, NOVL - 1).astype(jnp.int32),
        "coupling_coef": jnp.clip(jax.random.uniform(key_list[9], (PAIRS, NPART), jnp.float32, -0.4, 0.4) * level_of(key_list[9], (PAIRS, NPART), ((0, 512),), -0.4, 0.0), -0.4, 0.4),
        "margin_pool": noise(key_list[10], (NOVL * N_GRP, P_SIZE, P_SIZE), P_SIZE ** -0.5, 0.5, ((0, 32),)),
    }


def reference(int_table, dom_rows, pno_maps, amplitudes, pno_count, pno_energy, occ_sum, partner_slot, margin_index, coupling_coef, margin_pool):
    slab_total = N_BLK * N_GRP
    positions = jnp.arange(P_SIZE, dtype=jnp.int32)
    highest = lax.Precision.HIGHEST

    def slab_work(slab):
        cycle_pos = slab // N_GRP
        group_pos = slab % N_GRP
        first_pair = (slab * PAIRS_DEV).astype(jnp.int32)
        domain = lax.dynamic_slice_in_dim(dom_rows, first_pair, PAIRS_DEV, 0)
        row_block = int_table[domain].astype(jnp.float32)
        pno_block = lax.dynamic_slice_in_dim(pno_maps, first_pair, PAIRS_DEV, 0).astype(jnp.float32)
        projected = jnp.einsum("pqv,pva->pqa", row_block, pno_block, precision=highest).astype(jnp.bfloat16)
        proj_wide = lax.optimization_barrier(projected).astype(jnp.float32)
        exchange_k = jnp.einsum("pqa,pqb->pab", proj_wide, proj_wide, precision=highest)
        slot_ids = lax.dynamic_slice_in_dim(partner_slot, first_pair, PAIRS_DEV, 0)
        neighbour = (cycle_pos + slot_ids // PAIRS_DEV - 1) % N_BLK
        partner_pair = ((neighbour * N_GRP + group_pos) * PAIRS_DEV + slot_ids % PAIRS_DEV).astype(jnp.int32)
        partner_count = pno_count[partner_pair]
        partner_valid = (positions[None, None, :] < partner_count[:, :, None]).astype(jnp.float32)
        partner_tiles = amplitudes[partner_pair].astype(jnp.float32)
        partner_tiles = partner_tiles * partner_valid[:, :, :, None] * partner_valid[:, :, None, :]
        block_ovl = lax.dynamic_slice_in_dim(margin_index, first_pair, PAIRS_DEV, 0)
        margins = margin_pool[(group_pos * NOVL + block_ovl).astype(jnp.int32)].astype(jnp.float32)
        half_done = jnp.einsum("pmab,pmbc->pmac", margins, partner_tiles, precision=highest).astype(jnp.bfloat16)
        half_wide = lax.optimization_barrier(half_done).astype(jnp.float32)
        products = jnp.einsum("pmac,pmdc->pmad", half_wide, margins, precision=highest)
        weights = lax.dynamic_slice_in_dim(coupling_coef, first_pair, PAIRS_DEV, 0)
        coupling = jnp.einsum("pm,pmad->pad", weights, products, precision=highest)
        own_count = lax.dynamic_slice_in_dim(pno_count, first_pair, PAIRS_DEV, 0)
        pno_valid = (positions[None, :] < own_count[:, None]).astype(jnp.float32)
        tile_mask = pno_valid[:, :, None] * pno_valid[:, None, :]
        energies = lax.dynamic_slice_in_dim(pno_energy, first_pair, PAIRS_DEV, 0)
        occupied = lax.dynamic_slice_in_dim(occ_sum, first_pair, PAIRS_DEV, 0)
        fock_shift = energies[:, :, None] + energies[:, None, :] - occupied[:, None, None]
        own_amp = lax.dynamic_slice_in_dim(amplitudes, first_pair, PAIRS_DEV, 0).astype(jnp.float32)
        summed = (exchange_k + fock_shift * own_amp + coupling) * tile_mask
        return summed.astype(jnp.bfloat16)

    result = lax.map(slab_work, jnp.arange(slab_total, dtype=jnp.int32))
    return result.reshape(PAIRS, P_SIZE, P_SIZE)
```

```python
import functools

import jax
import jax.numpy as jnp
from jax import lax
from jax.experimental import pallas as pl
from jax.experimental.pallas import tpu as pltpu
from jax.sharding import PartitionSpec as P

NY, NZ, NX = 8, 8, 4
AXES = ("blk", "grp")
SMEM = pl.BlockSpec(memory_space=pltpu.SMEM)
VMEM = pl.BlockSpec(memory_space=pltpu.VMEM)
ANY = pl.BlockSpec(memory_space=pl.ANY)

FETCH = ((4, 2, -2, 0), (3, -3, 1, -1))


def device(y, q, z, x):
    return ((y % NY) * 2 + q) * NZ * NX + (z % NZ) * NX + x % NX


def moves(source):
    places = [(y, q, z, x) for y in range(NY) for q in range(2) for z in range(NZ) for x in range(NX)]
    return [(device(*source(*p)), device(*p)) for p in places]


def fetch_from(step):
    def source(y, q, z, x):
        row = (z + FETCH[q][step]) % NZ
        return y, q, row, x + y + 2 * z - 2 * row + row // 2

    return moves(source)


FETCHES = [fetch_from(step) for step in range(4)]
FROM_NEXT = moves(lambda y, q, z, x: (y, q, z, x + 1) if q == 0 else (y + 1, q, z, x))
FROM_PREVIOUS = moves(lambda y, q, z, x: (y, q, z, x - 1) if q == 0 else (y - 1, q, z, x))
FROM_SIDES = moves(lambda y, q, z, x: (y, q, z + 1, x) if q == 0 else (y, q, z - 1, x))
SWAP = moves(lambda y, q, z, x: (y, 1 - q, z, x))
OUTSIDE = moves(lambda y, q, z, x: (y - 1, 1, z, x) if q == 0 else (y + 1, 0, z, x))


def send(array, pattern):
    return lax.ppermute(array, AXES, pattern)


def spread(own):
    held = [own] + [send(own, pattern) for pattern in (FROM_NEXT, FROM_PREVIOUS, FROM_SIDES)]
    return held + [send(part, SWAP) for part in held]


def places_of(row_ids, shard_rows, y, q, z, x):
    group = row_ids // shard_rows
    row, column = group // NX, group % NX
    step = (column + 2 * row - row // 2 - (x + y + 2 * z)) & 3
    sideways = step == 2
    core = (row - z - sideways.astype(jnp.int32)) & 1
    holder = jnp.where(sideways, jnp.where(core == 0, z + 1, z - 1), z)
    away = (row - holder) & 7
    even = jnp.where(away == 4, 0, jnp.where(away == 2, 1, jnp.where(away == 6, 2, 3)))
    odd = jnp.where(away == 3, 0, jnp.where(away == 5, 1, jnp.where(away == 1, 2, 3)))
    spot = jnp.where(core == 0, even, odd)
    array = jnp.where(step == 0, 0, jnp.where(step == 1, 1, jnp.where(step == 3, 2, 3)))
    return (((core ^ q) * 4 + array) * 4 + spot) * shard_rows + row_ids % shard_rows


def exchange_kernel(pieces, place_ref, count_ref, maps_ref, rest_ref, *refs):
    piece_refs = refs[:pieces]
    out_ref, table_ref, picked, sems = refs[pieces:]
    depth = piece_refs[0].shape[0]
    copies = [
        pltpu.make_async_copy(piece, table_ref.at[pl.ds(i * depth, depth)], sems.at[i])
        for i, piece in enumerate(piece_refs)
    ]
    for copy in copies:
        copy.start()
    for copy in copies:
        copy.wait()
    pairs, _, tile = maps_ref.shape
    domain = place_ref.shape[0] // pairs
    unroll = 32

    @pl.loop(0, pairs * domain // unroll)
    def _(block):
        first = pl.multiple_of(block * 2 * unroll, 2 * unroll)
        for i in range(unroll):
            row = table_ref[place_ref[block * unroll + i]]
            picked[pl.ds(first + 2 * i, 2), :] = row.astype(jnp.float32)

    rows_at = lax.broadcasted_iota(jnp.int32, (tile, tile), 0)
    columns_at = lax.broadcasted_iota(jnp.int32, (tile, tile), 1)
    together = 4

    @pl.loop(0, pairs // together)
    def _(block):
        projected = []
        for i in range(together):
            pair = block * together + i
            first = pl.multiple_of(pair * 2 * domain, 2 * domain)
            low = picked[pl.ds(first, domain, stride=2), :].astype(jnp.bfloat16)
            high = picked[pl.ds(first + 1, domain, stride=2), :].astype(jnp.bfloat16)
            rows = jnp.concatenate([low, high], axis=1)
            projected.append(
                jnp.dot(rows, maps_ref[pair], preferred_element_type=jnp.float32).astype(jnp.bfloat16)
            )
        for i in range(together):
            pair = block * together + i
            gram = lax.dot_general(
                projected[i], projected[i], (((0,), (0,)), ((), ())), preferred_element_type=jnp.float32
            )
            count = count_ref[pair]
            valid = jnp.logical_and(rows_at < count, columns_at < count)
            out_ref[pair] = jnp.where(valid, gram + rest_ref[pair], 0.0).astype(jnp.bfloat16)


def exchange(place, counts, maps, rest, pieces):
    pairs, width, tile = maps.shape
    table_rows = sum(piece.shape[0] for piece in pieces)
    return pl.pallas_call(
        functools.partial(exchange_kernel, len(pieces)),
        out_shape=jax.ShapeDtypeStruct((pairs, tile, tile), jnp.bfloat16),
        in_specs=[SMEM, SMEM, VMEM, VMEM] + [ANY] * len(pieces),
        out_specs=VMEM,
        scratch_shapes=[
            pltpu.VMEM((table_rows, 2, width // 2), jnp.bfloat16),
            pltpu.VMEM((place.shape[0] * 2, width // 2), jnp.float32),
            pltpu.SemaphoreType.DMA((len(pieces),)),
        ],
        compiler_params=pltpu.CompilerParams(vmem_limit_bytes=32 * 2**20),
        cost_estimate=pl.CostEstimate(flops=10**9, bytes_accessed=30 * 2**20, transcendentals=0),
    )(place, counts, maps, rest, *pieces)


def couple_kernel(
    slot_ref, margin_ref, coef_ref, occ_ref, energy_ref, outside_ref, own_ref, partner_ref, pool_ref, out_ref, window, sems
):
    pairs, parts = slot_ref.shape
    tile = own_ref.shape[1]
    copies = [
        pltpu.make_async_copy(tiles, window.at[pl.ds(i * pairs, pairs)], sems.at[i])
        for i, tiles in enumerate((outside_ref, own_ref, partner_ref))
    ]
    for copy in copies:
        copy.start()
    for copy in copies:
        copy.wait()
    together = 2

    @pl.loop(0, pairs // together)
    def _(block):
        halves = []
        for i in range(together):
            pair = block * together + i
            for m in range(parts):
                margin = pool_ref[margin_ref[pair, m]]
                half = jnp.dot(margin, window[slot_ref[pair, m]], preferred_element_type=jnp.float32)
                halves.append((half.astype(jnp.bfloat16), margin))
        for i in range(together):
            pair = block * together + i
            energy = jnp.broadcast_to(energy_ref[pl.ds(pair, 1), :], (tile, tile))
            shift = energy + jnp.swapaxes(energy, 0, 1) - occ_ref[pair]
            total = shift * window[pairs + pair].astype(jnp.float32)
            for m in range(parts):
                half, margin = halves[i * parts + m]
                product = lax.dot_general(
                    half, margin, (((1,), (1,)), ((), ())), preferred_element_type=jnp.float32
                )
                total += coef_ref[pair, m] * product
            out_ref[pair] = total


def couple(slot, margin, coef, occ, energy, outside, own, partner, pool):
    pairs, tile, _ = own.shape
    return pl.pallas_call(
        couple_kernel,
        out_shape=jax.ShapeDtypeStruct((pairs, tile, tile), jnp.float32),
        in_specs=[SMEM] * 4 + [VMEM] + [ANY] * 3 + [VMEM],
        out_specs=VMEM,
        scratch_shapes=[
            pltpu.VMEM((3 * pairs, tile, tile), jnp.bfloat16),
            pltpu.SemaphoreType.DMA((3,)),
        ],
        compiler_params=pltpu.CompilerParams(vmem_limit_bytes=16 * 2**20),
        cost_estimate=pl.CostEstimate(flops=10**9, bytes_accessed=20 * 2**20, transcendentals=0),
    )(slot, margin, coef, occ, energy, outside, own, partner, pool)


def per_device(
    int_table,
    dom_rows,
    pno_maps,
    amplitudes,
    pno_count,
    pno_energy,
    occ_sum,
    partner_slot,
    margin_index,
    coupling_coef,
    margin_pool,
):
    shard_rows, width = int_table.shape
    pairs, tile, _ = amplitudes.shape
    blk, grp = lax.axis_index("blk"), lax.axis_index("grp")
    y, q, z, x = blk // 2, blk % 2, grp // NX, grp % NX

    shard = int_table.reshape(shard_rows, 2, width // 2)
    valid = jnp.arange(tile, dtype=jnp.int32)[None, :] < pno_count[:, None]
    mask = jnp.logical_and(valid[:, :, None], valid[:, None, :])
    masked = jnp.where(mask, amplitudes, jnp.zeros_like(amplitudes))

    fetched = [send(shard, pattern) for pattern in FETCHES[:2]]
    shard, masked = lax.optimization_barrier((shard, masked))
    outside = send(masked, OUTSIDE)
    fetched += [send(shard, pattern) for pattern in FETCHES[2:]]
    partner = send(masked, SWAP)
    part = partner_slot // pairs
    slot = jnp.where(q == 0, part, 2 - part) * pairs + partner_slot % pairs
    rest = couple(
        slot, margin_index, coupling_coef, occ_sum, pno_energy, outside, masked, partner, margin_pool
    )
    place = places_of(dom_rows, shard_rows, y, q, z, x).reshape(-1)
    fetched, rest, place = lax.optimization_barrier((fetched, rest, place))
    return exchange(place, pno_count, pno_maps, rest, spread(jnp.concatenate(fetched, axis=0)))


def solution(mesh):
    pairs = P(AXES)
    return jax.shard_map(
        per_device,
        mesh=mesh,
        in_specs=(P("grp"),) + (pairs,) * 9 + (P("grp"),),
        out_specs=pairs,
        check_vma=False,
    )
```

```python
import functools

import jax
import jax.numpy as jnp
from jax import lax
from jax.experimental import pallas as pl
from jax.experimental.pallas import tpu as pltpu
from jax.sharding import PartitionSpec as P

NY, NZ, NX = 8, 8, 4
AXES = ("blk", "grp")
SMEM = pl.BlockSpec(memory_space=pltpu.SMEM)
VMEM = pl.BlockSpec(memory_space=pltpu.VMEM)
ANY = pl.BlockSpec(memory_space=pl.ANY)
HBM = pl.BlockSpec(memory_space=pltpu.HBM)

FETCH = ((0, 2), (1, 3))
TILT = 2


def device(y, q, z, x):
    return ((y % NY) * 2 + q) * NZ * NX + (z % NZ) * NX + x % NX


def moves(source):
    places = [(y, q, z, x) for y in range(NY) for q in range(2) for z in range(NZ) for x in range(NX)]
    return [(device(*source(*p)), device(*p)) for p in places]


def fetch_from(step):
    def source(y, q, z, x):
        colour = (2 * x + y + 3 * z) % 8
        number = (z // 2 + FETCH[q][step]) % 4
        return y, q, 2 * number + colour % 2, colour // 2 + TILT * number

    return moves(source)


FETCHES = [fetch_from(step) for step in range(2)]
FROM_X = moves(lambda y, q, z, x: (y, q, z, x + 1 - 2 * q))
FROM_Y = moves(lambda y, q, z, x: (y + 1 - 2 * q, q, z, x))
FROM_Z = moves(lambda y, q, z, x: (y, q, z + 1 - 2 * q, x))
FROM_YZ = moves(lambda y, q, z, x: (y + 1 - 2 * q, q, z + 1 - 2 * q, x))
SWAP = moves(lambda y, q, z, x: (y, 1 - q, z, x))
OUTSIDE = moves(lambda y, q, z, x: (y - 1, 1, z, x) if q == 0 else (y + 1, 0, z, x))


def send(array, pattern):
    return lax.ppermute(array, AXES, pattern)


def places_of(row_ids, shard_rows, y, q, z, x):
    group = row_ids // shard_rows
    row, column = group // NX, group % NX
    number = row // 2
    step = (2 * ((column - TILT * number) & 3) + row % 2 - (2 * x + y + 3 * z)) & 7
    after, before = ((z + 1) & 7) // 2, ((z - 1) & 7) // 2
    from_before = (step > 4) | ((step == 4) & (((number - after) & 1) == 1))
    sideways = (step >= 3) & (step <= 5)
    holder = jnp.where(sideways, jnp.where(from_before, before, after), z // 2)
    turn = (number - holder) & 3
    spot = jnp.where(turn == 0, 0, jnp.where(turn == 2, 1, jnp.where(turn == 1, 2, 3)))
    far = jnp.minimum(step, 8 - step)
    array = jnp.where(far == 2, 0, jnp.where(far == 1, 4, jnp.where(far == 3, 8, 12)))
    first = jnp.where(step == 0, 0, 4 + (from_before.astype(jnp.int32) ^ q) * 14 + array)
    return (first + spot) * shard_rows + row_ids % shard_rows


def join_kernel(count, *refs):
    piece_refs, (out_ref, sems) = refs[:count], refs[-2:]
    depth = piece_refs[0].shape[0]
    copies = [
        pltpu.make_async_copy(piece, out_ref.at[pl.ds(i * depth, depth)], sems.at[i])
        for i, piece in enumerate(piece_refs)
    ]
    for copy in copies:
        copy.start()
    for copy in copies:
        copy.wait()


def join(pieces, after):
    depth, halves, width = pieces[0].shape
    return pl.pallas_call(
        functools.partial(join_kernel, len(pieces)),
        out_shape=jax.ShapeDtypeStruct((len(pieces) * depth, halves, width), pieces[0].dtype),
        in_specs=[ANY] * (len(pieces) + len(after)),
        out_specs=ANY,
        scratch_shapes=[pltpu.SemaphoreType.DMA((len(pieces),))],
        compiler_params=pltpu.CompilerParams(vmem_limit_bytes=2**20),
        cost_estimate=pl.CostEstimate(flops=0, bytes_accessed=2 * 2**20, transcendentals=0),
    )(*pieces, *after)


def merge_kernel(core_ref, own_ref, partner_ref, both_ref, first_ref, sems):
    depth = own_ref.shape[0]
    core = core_ref[0]
    copies = [
        pltpu.make_async_copy(own_ref, both_ref.at[pl.ds(core * depth, depth)], sems.at[0]),
        pltpu.make_async_copy(partner_ref, both_ref.at[pl.ds((1 - core) * depth, depth)], sems.at[1]),
    ]
    from_own = pltpu.make_async_copy(own_ref, first_ref, sems.at[2])
    from_partner = pltpu.make_async_copy(partner_ref, first_ref, sems.at[2])
    for copy in copies:
        copy.start()

    @pl.when(core == 0)
    def _():
        from_own.start()

    @pl.when(core == 1)
    def _():
        from_partner.start()

    for copy in copies:
        copy.wait()
    from_own.wait()


def merge(core, own, partner):
    depth, halves, width = own.shape
    return pl.pallas_call(
        merge_kernel,
        out_shape=[
            jax.ShapeDtypeStruct((2 * depth, halves, width), own.dtype),
            jax.ShapeDtypeStruct(own.shape, own.dtype),
        ],
        in_specs=[SMEM, ANY, ANY],
        out_specs=[ANY, ANY],
        scratch_shapes=[pltpu.SemaphoreType.DMA((3,))],
        compiler_params=pltpu.CompilerParams(vmem_limit_bytes=2**20),
        cost_estimate=pl.CostEstimate(flops=0, bytes_accessed=3 * 2**20, transcendentals=0),
    )(core, own, partner)


def exchange_kernel(pieces, place_ref, count_ref, maps_ref, rest_ref, *refs):
    piece_refs = refs[:pieces]
    out_ref, table_ref, picked, sems = refs[pieces:]
    copies, depth = [], 0
    for i, piece in enumerate(piece_refs):
        rows = table_ref.at[pl.ds(depth, piece.shape[0])]
        copies.append(pltpu.make_async_copy(piece, rows, sems.at[i]))
        depth += piece.shape[0]
    for copy in copies:
        copy.start()
    for copy in copies:
        copy.wait()
    pairs, _, tile = maps_ref.shape
    domain = place_ref.shape[0] // pairs
    unroll = 32

    @pl.loop(0, pairs * domain // unroll)
    def _(block):
        first = pl.multiple_of(block * 2 * unroll, 2 * unroll)
        for i in range(unroll):
            row = table_ref[place_ref[block * unroll + i]]
            picked[pl.ds(first + 2 * i, 2), :] = row.astype(jnp.float32)

    rows_at = lax.broadcasted_iota(jnp.int32, (tile, tile), 0)
    columns_at = lax.broadcasted_iota(jnp.int32, (tile, tile), 1)
    together = 4

    @pl.loop(0, pairs // together)
    def _(block):
        projected = []
        for i in range(together):
            pair = block * together + i
            first = pl.multiple_of(pair * 2 * domain, 2 * domain)
            low = picked[pl.ds(first, domain, stride=2), :].astype(jnp.bfloat16)
            high = picked[pl.ds(first + 1, domain, stride=2), :].astype(jnp.bfloat16)
            rows = jnp.concatenate([low, high], axis=1)
            projected.append(
                jnp.dot(rows, maps_ref[pair], preferred_element_type=jnp.float32).astype(jnp.bfloat16)
            )
        for i in range(together):
            pair = block * together + i
            gram = lax.dot_general(
                projected[i], projected[i], (((0,), (0,)), ((), ())), preferred_element_type=jnp.float32
            )
            count = count_ref[pair]
            valid = jnp.logical_and(rows_at < count, columns_at < count)
            out_ref[pair] = jnp.where(valid, gram + rest_ref[pair], 0.0).astype(jnp.bfloat16)


def exchange(place, counts, maps, rest, pieces):
    pairs, width, tile = maps.shape
    table_rows = sum(piece.shape[0] for piece in pieces)
    return pl.pallas_call(
        functools.partial(exchange_kernel, len(pieces)),
        out_shape=jax.ShapeDtypeStruct((pairs, tile, tile), jnp.bfloat16),
        in_specs=[SMEM, SMEM, VMEM, VMEM] + [ANY] * len(pieces),
        out_specs=VMEM,
        scratch_shapes=[
            pltpu.VMEM((table_rows, 2, width // 2), jnp.bfloat16),
            pltpu.VMEM((place.shape[0] * 2, width // 2), jnp.float32),
            pltpu.SemaphoreType.DMA((len(pieces),)),
        ],
        compiler_params=pltpu.CompilerParams(vmem_limit_bytes=18 * 2**20),
        cost_estimate=pl.CostEstimate(flops=10**9, bytes_accessed=30 * 2**20, transcendentals=0),
    )(place, counts, maps, rest, *pieces)


def mask_kernel(count_ref, tiles_ref, after_ref, out_ref, tiles, sem):
    pairs, tile, _ = tiles.shape
    copy = pltpu.make_async_copy(tiles_ref, tiles, sem)
    copy.start()
    copy.wait()
    rows_at = lax.broadcasted_iota(jnp.int32, (tile, tile), 0)
    columns_at = lax.broadcasted_iota(jnp.int32, (tile, tile), 1)
    for pair in range(pairs):
        count = count_ref[pair]
        valid = jnp.logical_and(rows_at < count, columns_at < count)
        out_ref[pair] = jnp.where(valid, tiles[pair].astype(jnp.float32), 0.0).astype(jnp.bfloat16)


def mask(counts, tiles, after):
    return pl.pallas_call(
        mask_kernel,
        out_shape=jax.ShapeDtypeStruct(tiles.shape, tiles.dtype),
        in_specs=[SMEM, HBM, ANY],
        out_specs=VMEM,
        scratch_shapes=[pltpu.VMEM(tiles.shape, tiles.dtype), pltpu.SemaphoreType.DMA(())],
        compiler_params=pltpu.CompilerParams(vmem_limit_bytes=4 * 2**20),
        cost_estimate=pl.CostEstimate(flops=10**6, bytes_accessed=2**20, transcendentals=0),
    )(counts, tiles, after)


def couple_kernel(
    core_ref,
    slot_hbm,
    margin_hbm,
    coef_hbm,
    occ_hbm,
    energy_hbm,
    pool_hbm,
    outside_ref,
    own_ref,
    partner_ref,
    out_ref,
    slot_ref,
    margin_ref,
    coef_ref,
    occ_ref,
    energy_ref,
    pool_ref,
    window,
    sems,
):
    parts, pairs = slot_hbm.shape
    tile = own_ref.shape[1]
    ends = [
        (outside_ref, window.at[pl.ds(0, pairs)]),
        (own_ref, window.at[pl.ds(pairs, pairs)]),
        (partner_ref, window.at[pl.ds(2 * pairs, pairs)]),
        (pool_hbm, pool_ref),
        (slot_hbm, slot_ref),
        (margin_hbm, margin_ref),
        (coef_hbm, coef_ref),
        (occ_hbm, occ_ref),
        (energy_hbm, energy_ref),
    ]
    copies = [pltpu.make_async_copy(*end, sems.at[i]) for i, end in enumerate(ends)]
    for copy in copies:
        copy.start()
    for copy in copies:
        copy.wait()
    core = core_ref[0]
    together = 2

    @pl.loop(0, pairs // together)
    def _(block):
        halves = []
        for i in range(together):
            pair = block * together + i
            for m in range(parts):
                margin = pool_ref[margin_ref[m, pair]]
                slot = slot_ref[m, pair]
                part, rest = slot // pairs, slot % pairs
                place = jnp.where(core == 0, part, 2 - part) * pairs + rest
                half = jnp.dot(margin, window[place], preferred_element_type=jnp.float32)
                halves.append((half.astype(jnp.bfloat16), margin))
        for i in range(together):
            pair = block * together + i
            energy = jnp.broadcast_to(energy_ref[pl.ds(pair, 1), :], (tile, tile))
            shift = energy + jnp.swapaxes(energy, 0, 1) - occ_ref[pair]
            total = shift * window[pairs + pair].astype(jnp.float32)
            for m in range(parts):
                half, margin = halves[i * parts + m]
                product = lax.dot_general(
                    half, margin, (((1,), (1,)), ((), ())), preferred_element_type=jnp.float32
                )
                total += coef_ref[m, pair] * product
            out_ref[pair] = total


def couple(core, slot, margin, coef, occ, energy, pool, outside, own, partner):
    pairs, tile, _ = own.shape
    small = [slot, margin, coef, occ]
    return pl.pallas_call(
        couple_kernel,
        out_shape=jax.ShapeDtypeStruct((pairs, tile, tile), jnp.float32),
        in_specs=[SMEM] + [HBM] * 6 + [ANY] * 3,
        out_specs=VMEM,
        scratch_shapes=[pltpu.SMEM(array.shape, array.dtype) for array in small]
        + [
            pltpu.VMEM(energy.shape, energy.dtype),
            pltpu.VMEM(pool.shape, pool.dtype),
            pltpu.VMEM((3 * pairs, tile, tile), jnp.bfloat16),
            pltpu.SemaphoreType.DMA((9,)),
        ],
        compiler_params=pltpu.CompilerParams(vmem_limit_bytes=8 * 2**20),
        cost_estimate=pl.CostEstimate(flops=10**9, bytes_accessed=20 * 2**20, transcendentals=0),
    )(core, *small, energy, pool, outside, own, partner)


def per_device(
    int_table,
    dom_rows,
    pno_maps,
    amplitudes,
    pno_count,
    pno_energy,
    occ_sum,
    partner_slot,
    margin_index,
    coupling_coef,
    margin_pool,
):
    shard_rows, width = int_table.shape
    blk, grp = lax.axis_index("blk"), lax.axis_index("grp")
    y, q, z, x = blk // 2, blk % 2, grp // NX, grp % NX

    shard = int_table.reshape(shard_rows, 2, width // 2)
    masked = mask(pno_count, amplitudes, shard)
    fetched = [send(shard, pattern) for pattern in FETCHES]
    outside, partner = send(masked, OUTSIDE), send(masked, SWAP)
    place = places_of(dom_rows, shard_rows, y, q, z, x).reshape(-1)
    core = q.reshape(1)
    rest = couple(
        core,
        partner_slot.T,
        margin_index.T,
        coupling_coef.T,
        occ_sum,
        pno_energy,
        margin_pool,
        outside,
        masked,
        partner,
    )
    own = join(fetched, (rest, place))
    both, first = merge(core, own, send(own, SWAP))
    held = [send(both, FROM_X), send(both, FROM_Y), send(both, FROM_Z), send(first, FROM_YZ)]
    pieces = [both] + held + [send(part, SWAP) for part in held]
    return exchange(place, pno_count, pno_maps, rest, pieces)


def solution(mesh):
    pairs = P(AXES)
    return jax.shard_map(
        per_device,
        mesh=mesh,
        in_specs=(P("grp"),) + (pairs,) * 9 + (P("grp"),),
        out_specs=pairs,
        check_vma=False,
    )
```

```python
import functools

import jax
import jax.numpy as jnp
from jax import lax
from jax.experimental import pallas as pl
from jax.experimental.pallas import tpu as pltpu
from jax.sharding import PartitionSpec as P

NY, NZ, NX = 8, 8, 4
AXES = ("blk", "grp")
SMEM = pl.BlockSpec(memory_space=pltpu.SMEM)
VMEM = pl.BlockSpec(memory_space=pltpu.VMEM)
ANY = pl.BlockSpec(memory_space=pl.ANY)
HBM = pl.BlockSpec(memory_space=pltpu.HBM)

FETCH = ((0, 2), (1, 3))
TILT = 2


def device(y, q, z, x):
    return ((y % NY) * 2 + q) * NZ * NX + (z % NZ) * NX + x % NX


def moves(source):
    places = [(y, q, z, x) for y in range(NY) for q in range(2) for z in range(NZ) for x in range(NX)]
    return [(device(*source(*p)), device(*p)) for p in places]


def fetch_from(step):
    def source(y, q, z, x):
        colour = (2 * x + y + 3 * z) % 8
        number = (z // 2 + FETCH[q][step]) % 4
        return y, q, 2 * number + colour % 2, colour // 2 + TILT * number

    return moves(source)


FETCHES = [fetch_from(step) for step in range(2)]
FROM_X = moves(lambda y, q, z, x: (y, q, z, x + 1 - 2 * q))
FROM_Y = moves(lambda y, q, z, x: (y + 1 - 2 * q, q, z, x))
FROM_Z = moves(lambda y, q, z, x: (y, q, z + 1 - 2 * q, x))
FROM_YZ = moves(lambda y, q, z, x: (y + 1 - 2 * q, q, z + 1 - 2 * q, x))
SWAP = moves(lambda y, q, z, x: (y, 1 - q, z, x))
OUTSIDE = moves(lambda y, q, z, x: (y - 1, 1, z, x) if q == 0 else (y + 1, 0, z, x))


def send(array, pattern):
    return lax.ppermute(array, AXES, pattern)


def places_of(row_ids, shard_rows, y, q, z, x):
    group = row_ids // shard_rows
    row, column = group // NX, group % NX
    number = row // 2
    step = (2 * ((column - TILT * number) & 3) + row % 2 - (2 * x + y + 3 * z)) & 7
    after, before = ((z + 1) & 7) // 2, ((z - 1) & 7) // 2
    from_before = (step > 4) | ((step == 4) & (((number - after) & 1) == 1))
    sideways = (step >= 3) & (step <= 5)
    holder = jnp.where(sideways, jnp.where(from_before, before, after), z // 2)
    turn = (number - holder) & 3
    spot = jnp.where(turn == 0, 0, jnp.where(turn == 2, 1, jnp.where(turn == 1, 2, 3)))
    far = jnp.minimum(step, 8 - step)
    array = jnp.where(far == 2, 0, jnp.where(far == 1, 4, jnp.where(far == 3, 8, 12)))
    first = jnp.where(step == 0, 0, 4 + (from_before.astype(jnp.int32) ^ q) * 14 + array)
    return (first + spot) * shard_rows + row_ids % shard_rows


def join_kernel(count, *refs):
    piece_refs, (out_ref, sems) = refs[:count], refs[-2:]
    depth = piece_refs[0].shape[0]
    copies = [
        pltpu.make_async_copy(piece, out_ref.at[pl.ds(i * depth, depth)], sems.at[i])
        for i, piece in enumerate(piece_refs)
    ]
    for copy in copies:
        copy.start()
    for copy in copies:
        copy.wait()


def join(pieces, after):
    depth, halves, width = pieces[0].shape
    return pl.pallas_call(
        functools.partial(join_kernel, len(pieces)),
        out_shape=jax.ShapeDtypeStruct((len(pieces) * depth, halves, width), pieces[0].dtype),
        in_specs=[ANY] * (len(pieces) + len(after)),
        out_specs=ANY,
        scratch_shapes=[pltpu.SemaphoreType.DMA((len(pieces),))],
        compiler_params=pltpu.CompilerParams(vmem_limit_bytes=2**20),
        cost_estimate=pl.CostEstimate(flops=0, bytes_accessed=2 * 2**20, transcendentals=0),
    )(*pieces, *after)


def once_kernel(array_ref, after_ref, out_ref):
    pass


def once(array, after):
    return pl.pallas_call(
        once_kernel,
        out_shape=jax.ShapeDtypeStruct(array.shape, array.dtype),
        in_specs=[ANY, ANY],
        out_specs=ANY,
        input_output_aliases={0: 0},
        compiler_params=pltpu.CompilerParams(vmem_limit_bytes=2**20),
    )(array, after)


def merge_kernel(core_ref, own_ref, partner_ref, *refs):
    both_ref, first_ref, sems = refs[-3:]
    depth = own_ref.shape[0]
    core = core_ref[0]
    copies = [
        pltpu.make_async_copy(own_ref, both_ref.at[pl.ds(core * depth, depth)], sems.at[0]),
        pltpu.make_async_copy(partner_ref, both_ref.at[pl.ds((1 - core) * depth, depth)], sems.at[1]),
    ]
    from_own = pltpu.make_async_copy(own_ref, first_ref, sems.at[2])
    from_partner = pltpu.make_async_copy(partner_ref, first_ref, sems.at[2])
    for copy in copies:
        copy.start()

    @pl.when(core == 0)
    def _():
        from_own.start()

    @pl.when(core == 1)
    def _():
        from_partner.start()

    for copy in copies:
        copy.wait()
    from_own.wait()


def merge(core, own, partner, after):
    depth, halves, width = own.shape
    return pl.pallas_call(
        merge_kernel,
        out_shape=[
            jax.ShapeDtypeStruct((2 * depth, halves, width), own.dtype),
            jax.ShapeDtypeStruct(own.shape, own.dtype),
        ],
        in_specs=[SMEM, ANY, ANY] + [ANY] * len(after),
        out_specs=[ANY, ANY],
        scratch_shapes=[pltpu.SemaphoreType.DMA((3,))],
        compiler_params=pltpu.CompilerParams(vmem_limit_bytes=2**20),
        cost_estimate=pl.CostEstimate(flops=0, bytes_accessed=3 * 2**20, transcendentals=0),
    )(core, own, partner, *after)


def exchange_kernel(pieces, place_ref, count_ref, maps_ref, rest_ref, *refs):
    piece_refs = refs[:pieces]
    out_ref, table_ref, picked, sems = refs[pieces:]
    copies, depth = [], 0
    for i, piece in enumerate(piece_refs):
        rows = table_ref.at[pl.ds(depth, piece.shape[0])]
        copies.append(pltpu.make_async_copy(piece, rows, sems.at[i]))
        depth += piece.shape[0]
    for copy in copies:
        copy.start()
    for copy in copies:
        copy.wait()
    pairs, _, tile = maps_ref.shape
    domain = place_ref.shape[0] // pairs
    unroll = 128

    @pl.loop(0, pairs * domain // unroll)
    def _(block):
        first = pl.multiple_of(block * 2 * unroll, 2 * unroll)
        for i in range(unroll):
            row = table_ref[place_ref[block * unroll + i]]
            picked[pl.ds(first + 2 * i, 2), :] = row.astype(jnp.float32)

    rows_at = lax.broadcasted_iota(jnp.int32, (tile, tile), 0)
    columns_at = lax.broadcasted_iota(jnp.int32, (tile, tile), 1)
    projected = []
    for pair in range(pairs):
        first = pair * 2 * domain
        low = picked[pl.ds(first, domain, stride=2), :].astype(jnp.bfloat16)
        high = picked[pl.ds(first + 1, domain, stride=2), :].astype(jnp.bfloat16)
        rows = jnp.concatenate([low, high], axis=1)
        projected.append(jnp.dot(rows, maps_ref[pair], preferred_element_type=jnp.float32).astype(jnp.bfloat16))
    for pair in range(pairs):
        gram = lax.dot_general(
            projected[pair], projected[pair], (((0,), (0,)), ((), ())), preferred_element_type=jnp.float32
        )
        count = count_ref[pair]
        valid = jnp.logical_and(rows_at < count, columns_at < count)
        out_ref[pair] = jnp.where(valid, gram + rest_ref[pair], 0.0).astype(jnp.bfloat16)


def exchange(place, counts, maps, rest, pieces):
    pairs, width, tile = maps.shape
    table_rows = sum(piece.shape[0] for piece in pieces)
    return pl.pallas_call(
        functools.partial(exchange_kernel, len(pieces)),
        out_shape=jax.ShapeDtypeStruct((pairs, tile, tile), jnp.bfloat16),
        in_specs=[SMEM, SMEM, VMEM, VMEM] + [ANY] * len(pieces),
        out_specs=VMEM,
        scratch_shapes=[
            pltpu.VMEM((table_rows, 2, width // 2), jnp.bfloat16),
            pltpu.VMEM((place.shape[0] * 2, width // 2), jnp.float32),
            pltpu.SemaphoreType.DMA((len(pieces),)),
        ],
        compiler_params=pltpu.CompilerParams(vmem_limit_bytes=24 * 2**20),
        cost_estimate=pl.CostEstimate(flops=10**9, bytes_accessed=30 * 2**20, transcendentals=0),
    )(place, counts, maps, rest, *pieces)


def mask_kernel(count_ref, tiles_ref, after_ref, out_ref, tiles, sem):
    pairs, tile, _ = tiles.shape
    copy = pltpu.make_async_copy(tiles_ref, tiles, sem)
    copy.start()
    copy.wait()
    rows_at = lax.broadcasted_iota(jnp.int32, (tile, tile), 0)
    columns_at = lax.broadcasted_iota(jnp.int32, (tile, tile), 1)
    for pair in range(pairs):
        count = count_ref[pair]
        valid = jnp.logical_and(rows_at < count, columns_at < count)
        out_ref[pair] = jnp.where(valid, tiles[pair].astype(jnp.float32), 0.0).astype(jnp.bfloat16)


def mask(counts, tiles, after):
    return pl.pallas_call(
        mask_kernel,
        out_shape=jax.ShapeDtypeStruct(tiles.shape, tiles.dtype),
        in_specs=[SMEM, HBM, ANY],
        out_specs=VMEM,
        scratch_shapes=[pltpu.VMEM(tiles.shape, tiles.dtype), pltpu.SemaphoreType.DMA(())],
        compiler_params=pltpu.CompilerParams(vmem_limit_bytes=4 * 2**20),
        cost_estimate=pl.CostEstimate(flops=10**6, bytes_accessed=2**20, transcendentals=0),
    )(counts, tiles, after)


def couple_kernel(
    core_ref,
    slot_hbm,
    margin_hbm,
    coef_hbm,
    occ_hbm,
    energy_hbm,
    pool_hbm,
    outside_ref,
    own_ref,
    partner_ref,
    after_ref,
    out_ref,
    slot_ref,
    margin_ref,
    coef_ref,
    occ_ref,
    energy_ref,
    pool_ref,
    window,
    sems,
):
    parts, pairs = slot_hbm.shape
    tile = own_ref.shape[1]
    ends = [
        (outside_ref, window.at[pl.ds(0, pairs)]),
        (own_ref, window.at[pl.ds(pairs, pairs)]),
        (partner_ref, window.at[pl.ds(2 * pairs, pairs)]),
        (pool_hbm, pool_ref),
        (slot_hbm, slot_ref),
        (margin_hbm, margin_ref),
        (coef_hbm, coef_ref),
        (occ_hbm, occ_ref),
        (energy_hbm, energy_ref),
    ]
    copies = [pltpu.make_async_copy(*end, sems.at[i]) for i, end in enumerate(ends)]
    for copy in copies:
        copy.start()
    for copy in copies:
        copy.wait()
    core = core_ref[0]
    together = 8

    @pl.loop(0, pairs // together)
    def _(block):
        halves = []
        for i in range(together):
            pair = block * together + i
            for m in range(parts):
                margin = pool_ref[margin_ref[m, pair]]
                slot = slot_ref[m, pair]
                part, rest = slot // pairs, slot % pairs
                place = jnp.where(core == 0, part, 2 - part) * pairs + rest
                half = jnp.dot(margin, window[place], preferred_element_type=jnp.float32)
                halves.append((half.astype(jnp.bfloat16), margin))
        for i in range(together):
            pair = block * together + i
            energy = jnp.broadcast_to(energy_ref[pl.ds(pair, 1), :], (tile, tile))
            shift = energy + jnp.swapaxes(energy, 0, 1) - occ_ref[pair]
            total = shift * window[pairs + pair].astype(jnp.float32)
            for m in range(parts):
                half, margin = halves[i * parts + m]
                product = lax.dot_general(
                    half, margin, (((1,), (1,)), ((), ())), preferred_element_type=jnp.float32
                )
                total += coef_ref[m, pair] * product
            out_ref[pair] = total


def couple(core, slot, margin, coef, occ, energy, pool, outside, own, partner, after):
    pairs, tile, _ = own.shape
    small = [slot, margin, coef, occ]
    return pl.pallas_call(
        couple_kernel,
        out_shape=jax.ShapeDtypeStruct((pairs, tile, tile), jnp.float32),
        in_specs=[SMEM] + [HBM] * 6 + [ANY] * 4,
        out_specs=VMEM,
        scratch_shapes=[pltpu.SMEM(array.shape, array.dtype) for array in small]
        + [
            pltpu.VMEM(energy.shape, energy.dtype),
            pltpu.VMEM(pool.shape, pool.dtype),
            pltpu.VMEM((3 * pairs, tile, tile), jnp.bfloat16),
            pltpu.SemaphoreType.DMA((9,)),
        ],
        compiler_params=pltpu.CompilerParams(vmem_limit_bytes=16 * 2**20),
        cost_estimate=pl.CostEstimate(flops=10**9, bytes_accessed=20 * 2**20, transcendentals=0),
    )(core, *small, energy, pool, outside, own, partner, after)


def per_device(
    int_table,
    dom_rows,
    pno_maps,
    amplitudes,
    pno_count,
    pno_energy,
    occ_sum,
    partner_slot,
    margin_index,
    coupling_coef,
    margin_pool,
):
    shard_rows, width = int_table.shape
    blk, grp = lax.axis_index("blk"), lax.axis_index("grp")
    y, q, z, x = blk // 2, blk % 2, grp // NX, grp % NX

    shard = int_table.reshape(shard_rows, 2, width // 2)
    masked = mask(pno_count, amplitudes, shard)
    fetched = [send(shard, pattern) for pattern in FETCHES]
    outside, partner = send(masked, OUTSIDE), send(masked, SWAP)
    place = places_of(dom_rows, shard_rows, y, q, z, x).reshape(-1)
    core = q.reshape(1)
    own = join(fetched, (place,))
    both, first = merge(core, own, send(own, SWAP), (outside, partner))
    held = [send(both, FROM_X), send(both, FROM_Y), send(both, FROM_Z), send(first, FROM_YZ)]
    rest = couple(
        core,
        partner_slot.T,
        margin_index.T,
        coupling_coef.T,
        occ_sum,
        pno_energy,
        margin_pool,
        outside,
        masked,
        partner,
        both,
    )
    held = [once(part, rest) for part in held]
    pieces = [both] + held + [send(part, SWAP) for part in held]
    return exchange(place, pno_count, pno_maps, rest, pieces)


def solution(mesh):
    pairs = P(AXES)
    return jax.shard_map(
        per_device,
        mesh=mesh,
        in_specs=(P("grp"),) + (pairs,) * 9 + (P("grp"),),
        out_specs=pairs,
        check_vma=False,
    )
```

```python
import functools

import jax
import jax.numpy as jnp
from jax import lax
from jax.experimental import pallas as pl
from jax.experimental.pallas import tpu as pltpu
from jax.sharding import PartitionSpec as P

NY, NZ, NX = 8, 8, 4
AXES = ("blk", "grp")
SMEM = pl.BlockSpec(memory_space=pltpu.SMEM)
VMEM = pl.BlockSpec(memory_space=pltpu.VMEM)
ANY = pl.BlockSpec(memory_space=pl.ANY)

FETCH = ((0, 2), (1, 3))
TILT = 2


def device(y, q, z, x):
    return ((y % NY) * 2 + q) * NZ * NX + (z % NZ) * NX + x % NX


def moves(source):
    places = [(y, q, z, x) for y in range(NY) for q in range(2) for z in range(NZ) for x in range(NX)]
    return [(device(*source(*p)), device(*p)) for p in places]


def fetch_from(step):
    def source(y, q, z, x):
        colour = (2 * x + y + 3 * z) % 8
        number = (z // 2 + FETCH[q][step]) % 4
        return y, q, 2 * number + colour % 2, colour // 2 + TILT * number

    return moves(source)


FETCHES = [fetch_from(step) for step in range(2)]
FROM_X = moves(lambda y, q, z, x: (y, q, z, x + 1 - 2 * q))
FROM_Y = moves(lambda y, q, z, x: (y + 1 - 2 * q, q, z, x))
FROM_Z = moves(lambda y, q, z, x: (y, q, z + 1 - 2 * q, x))
FROM_YZ = moves(lambda y, q, z, x: (y + 1 - 2 * q, q, z + 1 - 2 * q, x))
SWAP = moves(lambda y, q, z, x: (y, 1 - q, z, x))
OUTSIDE = moves(lambda y, q, z, x: (y - 1, 1, z, x) if q == 0 else (y + 1, 0, z, x))


def send(array, pattern):
    return lax.ppermute(array, AXES, pattern)


def places_of(row_ids, shard_rows, y, q, z, x):
    group = row_ids // shard_rows
    row, column = group // NX, group % NX
    number = row // 2
    step = (2 * ((column - TILT * number) & 3) + row % 2 - (2 * x + y + 3 * z)) & 7
    after, before = ((z + 1) & 7) // 2, ((z - 1) & 7) // 2
    from_before = (step > 4) | ((step == 4) & (((number - after) & 1) == 1))
    sideways = (step >= 3) & (step <= 5)
    holder = jnp.where(sideways, jnp.where(from_before, before, after), z // 2)
    turn = (number - holder) & 3
    spot = jnp.where(turn == 0, 0, jnp.where(turn == 2, 1, jnp.where(turn == 1, 2, 3)))
    far = jnp.minimum(step, 8 - step)
    array = jnp.where(far == 2, 0, jnp.where(far == 1, 4, jnp.where(far == 3, 8, 12)))
    first = jnp.where(step == 0, 0, 4 + (from_before.astype(jnp.int32) ^ q) * 14 + array)
    return (first + spot) * shard_rows + row_ids % shard_rows


def join_kernel(count, *refs):
    piece_refs, (out_ref, sems) = refs[:count], refs[-2:]
    depth = piece_refs[0].shape[0]
    copies = [
        pltpu.make_async_copy(piece, out_ref.at[pl.ds(i * depth, depth)], sems.at[i])
        for i, piece in enumerate(piece_refs)
    ]
    for copy in copies:
        copy.start()
    for copy in copies:
        copy.wait()


def join(pieces, after):
    depth, halves, width = pieces[0].shape
    return pl.pallas_call(
        functools.partial(join_kernel, len(pieces)),
        out_shape=jax.ShapeDtypeStruct((len(pieces) * depth, halves, width), pieces[0].dtype),
        in_specs=[ANY] * (len(pieces) + len(after)),
        out_specs=ANY,
        scratch_shapes=[pltpu.SemaphoreType.DMA((len(pieces),))],
        compiler_params=pltpu.CompilerParams(vmem_limit_bytes=2**20),
        cost_estimate=pl.CostEstimate(flops=0, bytes_accessed=2 * 2**20, transcendentals=0),
    )(*pieces, *after)


def once_kernel(array_ref, after_ref, out_ref):
    pass


def once(array, after):
    return pl.pallas_call(
        once_kernel,
        out_shape=jax.ShapeDtypeStruct(array.shape, array.dtype),
        in_specs=[ANY, ANY],
        out_specs=ANY,
        input_output_aliases={0: 0},
        compiler_params=pltpu.CompilerParams(vmem_limit_bytes=2**20),
    )(array, after)


def merge_kernel(core_ref, own_ref, partner_ref, *refs):
    both_ref, first_ref, sems = refs[-3:]
    depth = own_ref.shape[0]
    core = core_ref[0]
    copies = [
        pltpu.make_async_copy(own_ref, both_ref.at[pl.ds(core * depth, depth)], sems.at[0]),
        pltpu.make_async_copy(partner_ref, both_ref.at[pl.ds((1 - core) * depth, depth)], sems.at[1]),
    ]
    from_own = pltpu.make_async_copy(own_ref, first_ref, sems.at[2])
    from_partner = pltpu.make_async_copy(partner_ref, first_ref, sems.at[2])
    for copy in copies:
        copy.start()

    @pl.when(core == 0)
    def _():
        from_own.start()

    @pl.when(core == 1)
    def _():
        from_partner.start()

    for copy in copies:
        copy.wait()
    from_own.wait()


def merge(core, own, partner, after):
    depth, halves, width = own.shape
    return pl.pallas_call(
        merge_kernel,
        out_shape=[
            jax.ShapeDtypeStruct((2 * depth, halves, width), own.dtype),
            jax.ShapeDtypeStruct(own.shape, own.dtype),
        ],
        in_specs=[SMEM, ANY, ANY] + [ANY] * len(after),
        out_specs=[ANY, ANY],
        scratch_shapes=[pltpu.SemaphoreType.DMA((3,))],
        compiler_params=pltpu.CompilerParams(vmem_limit_bytes=2**20),
        cost_estimate=pl.CostEstimate(flops=0, bytes_accessed=3 * 2**20, transcendentals=0),
    )(core, own, partner, *after)


def exchange_kernel(pieces, place_ref, count_ref, maps_ref, rest_ref, *refs):
    piece_refs = refs[:pieces]
    out_ref, table_ref, picked, sems = refs[pieces:]
    copies, depth = [], 0
    for i, piece in enumerate(piece_refs):
        rows = table_ref.at[pl.ds(depth, piece.shape[0])]
        copies.append(pltpu.make_async_copy(piece, rows, sems.at[i]))
        depth += piece.shape[0]
    for copy in copies:
        copy.start()
    for copy in copies:
        copy.wait()
    pairs, _, tile = maps_ref.shape
    domain = place_ref.shape[0] // pairs
    unroll = 128

    @pl.loop(0, pairs * domain // unroll)
    def _(block):
        first = pl.multiple_of(block * 2 * unroll, 2 * unroll)
        for i in range(unroll):
            row = table_ref[place_ref[block * unroll + i]]
            picked[pl.ds(first + 2 * i, 2), :] = row.astype(jnp.float32)

    rows_at = lax.broadcasted_iota(jnp.int32, (tile, tile), 0)
    columns_at = lax.broadcasted_iota(jnp.int32, (tile, tile), 1)
    projected = []
    for pair in range(pairs):
        first = pair * 2 * domain
        low = picked[pl.ds(first, domain, stride=2), :].astype(jnp.bfloat16)
        high = picked[pl.ds(first + 1, domain, stride=2), :].astype(jnp.bfloat16)
        rows = jnp.concatenate([low, high], axis=1)
        projected.append(jnp.dot(rows, maps_ref[pair], preferred_element_type=jnp.float32).astype(jnp.bfloat16))
    for pair in range(pairs):
        gram = lax.dot_general(
            projected[pair], projected[pair], (((0,), (0,)), ((), ())), preferred_element_type=jnp.float32
        )
        count = count_ref[pair]
        valid = jnp.logical_and(rows_at < count, columns_at < count)
        out_ref[pair] = jnp.where(valid, gram + rest_ref[pair], 0.0).astype(jnp.bfloat16)


def exchange(place, counts, maps, rest, pieces):
    pairs, width, tile = maps.shape
    table_rows = sum(piece.shape[0] for piece in pieces)
    return pl.pallas_call(
        functools.partial(exchange_kernel, len(pieces)),
        out_shape=jax.ShapeDtypeStruct((pairs, tile, tile), jnp.bfloat16),
        in_specs=[SMEM, SMEM, VMEM, VMEM] + [ANY] * len(pieces),
        out_specs=VMEM,
        scratch_shapes=[
            pltpu.VMEM((table_rows, 2, width // 2), jnp.bfloat16),
            pltpu.VMEM((place.shape[0] * 2 + 16, width // 2), jnp.float32),
            pltpu.SemaphoreType.DMA((len(pieces),)),
        ],
        compiler_params=pltpu.CompilerParams(vmem_limit_bytes=24 * 2**20),
        cost_estimate=pl.CostEstimate(flops=10**9, bytes_accessed=30 * 2**20, transcendentals=0),
    )(place, counts, maps, rest, *pieces)


def mask_kernel(count_ref, tiles_ref, after_ref, out_ref, tiles, sem):
    pairs, tile, _ = tiles.shape
    copy = pltpu.make_async_copy(tiles_ref, tiles, sem)
    copy.start()
    copy.wait()
    rows_at = lax.broadcasted_iota(jnp.int32, (tile, tile), 0)
    columns_at = lax.broadcasted_iota(jnp.int32, (tile, tile), 1)
    for pair in range(pairs):
        count = count_ref[pair]
        valid = jnp.logical_and(rows_at < count, columns_at < count)
        out_ref[pair] = jnp.where(valid, tiles[pair].astype(jnp.float32), 0.0).astype(jnp.bfloat16)


def mask(counts, tiles, after):
    return pl.pallas_call(
        mask_kernel,
        out_shape=jax.ShapeDtypeStruct(tiles.shape, tiles.dtype),
        in_specs=[SMEM, ANY, ANY],
        out_specs=VMEM,
        scratch_shapes=[pltpu.VMEM(tiles.shape, tiles.dtype), pltpu.SemaphoreType.DMA(())],
        compiler_params=pltpu.CompilerParams(vmem_limit_bytes=4 * 2**20),
        cost_estimate=pl.CostEstimate(flops=10**6, bytes_accessed=2**20, transcendentals=0),
    )(counts, tiles, after)


def couple_kernel(
    core_ref,
    slot_hbm,
    margin_hbm,
    coef_hbm,
    occ_hbm,
    energy_hbm,
    pool_hbm,
    outside_ref,
    own_ref,
    partner_ref,
    after_ref,
    out_ref,
    slot_ref,
    margin_ref,
    coef_ref,
    occ_ref,
    energy_ref,
    pool_ref,
    window,
    sems,
):
    parts, pairs = slot_hbm.shape
    tile = own_ref.shape[1]
    ends = [
        (outside_ref, window.at[pl.ds(0, pairs)]),
        (own_ref, window.at[pl.ds(pairs, pairs)]),
        (partner_ref, window.at[pl.ds(2 * pairs, pairs)]),
        (pool_hbm, pool_ref),
        (slot_hbm, slot_ref),
        (margin_hbm, margin_ref),
        (coef_hbm, coef_ref),
        (occ_hbm, occ_ref),
        (energy_hbm, energy_ref),
    ]
    copies = [pltpu.make_async_copy(*end, sems.at[i]) for i, end in enumerate(ends)]
    for copy in copies:
        copy.start()
    for copy in copies:
        copy.wait()
    core = core_ref[0]
    together = 8

    @pl.loop(0, pairs // together)
    def _(block):
        halves = []
        for i in range(together):
            pair = block * together + i
            for m in range(parts):
                margin = pool_ref[margin_ref[m, pair]]
                slot = slot_ref[m, pair]
                part, rest = slot // pairs, slot % pairs
                place = jnp.where(core == 0, part, 2 - part) * pairs + rest
                half = jnp.dot(margin, window[place], preferred_element_type=jnp.float32)
                halves.append((half.astype(jnp.bfloat16), margin))
        for i in range(together):
            pair = block * together + i
            energy = jnp.broadcast_to(energy_ref[pl.ds(pair, 1), :], (tile, tile))
            shift = energy + jnp.swapaxes(energy, 0, 1) - occ_ref[pair]
            total = shift * window[pairs + pair].astype(jnp.float32)
            for m in range(parts):
                half, margin = halves[i * parts + m]
                product = lax.dot_general(
                    half, margin, (((1,), (1,)), ((), ())), preferred_element_type=jnp.float32
                )
                total += coef_ref[m, pair] * product
            out_ref[pair] = total


def couple(core, slot, margin, coef, occ, energy, pool, outside, own, partner, after):
    pairs, tile, _ = own.shape
    small = [slot, margin, coef, occ]
    return pl.pallas_call(
        couple_kernel,
        out_shape=jax.ShapeDtypeStruct((pairs, tile, tile), jnp.float32),
        in_specs=[SMEM] + [ANY] * 10,
        out_specs=VMEM,
        scratch_shapes=[pltpu.SMEM(array.shape, array.dtype) for array in small]
        + [
            pltpu.VMEM(energy.shape, energy.dtype),
            pltpu.VMEM(pool.shape, pool.dtype),
            pltpu.VMEM((3 * pairs, tile, tile), jnp.bfloat16),
            pltpu.SemaphoreType.DMA((9,)),
        ],
        compiler_params=pltpu.CompilerParams(vmem_limit_bytes=16 * 2**20),
        cost_estimate=pl.CostEstimate(flops=10**9, bytes_accessed=20 * 2**20, transcendentals=0),
    )(core, *small, energy, pool, outside, own, partner, after)


def per_device(
    int_table,
    dom_rows,
    pno_maps,
    amplitudes,
    pno_count,
    pno_energy,
    occ_sum,
    partner_slot,
    margin_index,
    coupling_coef,
    margin_pool,
):
    shard_rows, width = int_table.shape
    blk, grp = lax.axis_index("blk"), lax.axis_index("grp")
    y, q, z, x = blk // 2, blk % 2, grp // NX, grp % NX

    shard = int_table.reshape(shard_rows, 2, width // 2)
    masked = mask(pno_count, amplitudes, shard)
    fetched = [send(shard, pattern) for pattern in FETCHES]
    outside, partner = send(masked, OUTSIDE), send(masked, SWAP)
    place = places_of(dom_rows, shard_rows, y, q, z, x).reshape(-1)
    core = q.reshape(1)
    own = join(fetched, (place,))
    both, first = merge(core, own, send(own, SWAP), (outside, partner))
    held = [send(both, FROM_X), send(both, FROM_Y), send(both, FROM_Z), send(first, FROM_YZ)]
    rest = couple(
        core,
        partner_slot.T,
        margin_index.T,
        coupling_coef.T,
        occ_sum,
        pno_energy,
        margin_pool,
        outside,
        masked,
        partner,
        both,
    )
    held = [once(part, rest) for part in held]
    pieces = [both] + held + [send(part, SWAP) for part in held]
    return exchange(place, pno_count, pno_maps, rest, pieces)


def solution(mesh):
    pairs = P(AXES)
    return jax.shard_map(
        per_device,
        mesh=mesh,
        in_specs=(P("grp"),) + (pairs,) * 9 + (P("grp"),),
        out_specs=pairs,
        check_vma=False,
    )
```
